32 devices in a mesh: curve: 8 (over z, y), slab: 4 (over x, core).
Axes of the slice: x: 2, y: 2, z: 4, core: 2. Of those that a mesh axis runs over, the one named last changes fastest.
Arguments:
- state: float32 [5, 125, 4, 1024], P(None, None, 'slab', 'curve'), as said below
- levels: int32 [4, 1024], P('slab', 'curve'), may hold values from 0 to 2
- neighbours: int32 [6, 4, 1024], P(None, 'slab', 'curve'), may hold values from 0 to 4095, as said below
- shifts: int32 [4, 8], P('slab', 'curve'), may hold values from -32 to 32
Outputs:
- moved: float32 [5, 125, 4, 1024], P(None, None, 'slab', 'curve')
- mortar: float32 [5, 25, 4, 1024], P(None, None, 'slab', 'curve')
The draws below stay inside these ranges and needn't reach their ends.
Inputs may be any that keep to these rules, and one draw needn't show every extreme that they name: `neighbours`: faces 0 and 1 name an element of the row before and the row after (cyclically), faces 2 and 3 one of the same row; for faces 0 to 3 the named element sits in the same block of 128 positions; face 4 names one of the same row in the same block or the block before, face 5 in the same block or the block after (cyclically over blocks). `state`: density and pressure positive.
All inputs are finite; a program needn't handle non-finite values.
Results may differ from the reference program's by a relative error of at most 0.00021.
Values sent between devices are 32-bit elements; how exact they have to be, the bound alone decides.
A program may use at most 64 MiB of HBM per device.

```python
import jax
import jax.numpy as jnp
import numpy as np
from jax import lax

NV = 5
ORDER = 5
NODES = 125
FACE = 25
EL = 128
SHIFT_MAX = 32
ROWS = 4
BLOCKS = 8
ECURVE = 1024


GAMMA = 1.4


def draw_state(key, part):
    keys = jax.random.split(jax.random.fold_in(key, 11), 6)
    shape = (NODES, ROWS, ECURVE)
    density = jax.random.uniform(keys[1], shape, jnp.float32, 0.6, 1.6)
    velocity = 0.4 * jax.random.normal(keys[2], (3,) + shape, jnp.float32)
    press = jax.random.uniform(keys[4], shape, jnp.float32, 0.6, 1.6)
    momentum = density * velocity
    energy = press / (GAMMA - 1.0) + 0.5 * density * jnp.sum(velocity * velocity, axis=0)
    return jnp.concatenate([density[None], momentum, energy[None]], axis=0).astype(jnp.float32)


def draw_neighbours(key, part):
    keys = jax.random.split(jax.random.fold_in(key, 23), 2)
    offsets = jax.random.randint(keys[0], (6, ROWS, ECURVE), 0, EL)
    steps = jax.random.randint(keys[1], (2, ROWS, ECURVE), 0, 2)
    rows = jnp.arange(ROWS, dtype=jnp.int32)[:, None] + jnp.zeros((ROWS, ECURVE), jnp.int32)
    block = jnp.arange(ECURVE, dtype=jnp.int32)[None, :] // EL + jnp.zeros((ROWS, ECURVE), jnp.int32)
    row_of = [(rows - 1) % ROWS, (rows + 1) % ROWS, rows, rows, rows, rows]
    block_of = [block, block, block, block, (block - steps[0]) % BLOCKS, (block + steps[1]) % BLOCKS]
    lists = [row_of[f] * ECURVE + block_of[f] * EL + offsets[f] for f in range(6)]
    return jnp.stack(lists).astype(jnp.int32)


def draw_shifts(key, part):
    keys = jax.random.split(jax.random.fold_in(key, 37), 2)
    values = jax.random.randint(keys[0], (ROWS * BLOCKS,), -SHIFT_MAX, SHIFT_MAX + 1)
    chosen = jax.random.permutation(keys[1], ROWS * BLOCKS)
    values = values.at[chosen[0]].set(SHIFT_MAX).at[chosen[1]].set(-SHIFT_MAX)
    return values.reshape(ROWS, BLOCKS).astype(jnp.int32)


def with_ends(values, key, low, high):
    longest = values.shape.index(max(values.shape))
    spots = []
    for shift in (0, 1):
        where = [jax.random.randint(jax.random.fold_in(key, axis), (), 0, length) for axis, length in enumerate(values.shape)]
        where[longest] = (where[longest] + shift) % values.shape[longest]
        spots.append(tuple(where))
    return values.at[spots[0]].set(low).at[spots[1]].set(high)


def setup_inputs(seed: int = 0) -> dict:
    splits = jax.random.split(jax.random.key(seed), 5)
    state = draw_state(jax.random.fold_in(splits[4], 71), 0)
    levels = with_ends(jax.random.randint(splits[1], (ROWS, ECURVE), 0, 3), jax.random.fold_in(splits[1], 1), 0, 2).astype(jnp.int32)
    neighbours = draw_neighbours(jax.random.fold_in(splits[4], 71), 0)
    shifts = draw_shifts(jax.random.fold_in(splits[4], 71), 0)
    return {"state": state, "levels": levels, "neighbours": neighbours, "shifts": shifts}


GAMMA = 1.4
CFL = 0.05
END_WEIGHT = 0.1

def derivative_matrix():
    points = np.array([-1.0, -np.sqrt(3.0 / 7.0), 0.0, np.sqrt(3.0 / 7.0), 1.0])
    bary = np.array([1.0 / np.prod([points[j] - points[k] for k in range(5) if k != j]) for j in range(5)])
    table = np.zeros((5, 5))
    for i in range(5):
        for j in range(5):
            if i != j:
                table[i, j] = bary[j] / bary[i] / (points[i] - points[j])
        table[i, i] = -np.sum(table[i])
    return jnp.asarray(table, jnp.float32)

def euler_flux(u, d):
    density = u[0]
    momentum = u[1:4]
    energy = u[4]
    velocity = momentum / density
    press = (GAMMA - 1.0) * (energy - 0.5 * lax.optimization_barrier(jnp.sum(momentum * velocity, axis=0)))
    along = velocity[d]
    parts = [momentum[d]]
    for a in range(3):
        term = momentum[a] * along
        if a == d:
            term = term + press
        parts.append(term)
    parts.append((energy + press) * along)
    return jnp.stack(parts)

def wave_speed(u):
    velocity = u[1:4] / u[0]
    press = (GAMMA - 1.0) * (u[4] - 0.5 * lax.optimization_barrier(jnp.sum(u[1:4] * velocity, axis=0)))
    return jnp.sqrt(lax.optimization_barrier(jnp.sum(velocity * velocity, axis=0))) + jnp.sqrt(GAMMA * press / u[0])

def rusanov(lower, upper, d, lam):
    return 0.5 * (euler_flux(lower, d) + euler_flux(upper, d)) - 0.5 * lam * (upper - lower)

def own_faces(u5):
    return [u5[:, :, :, 0], u5[:, :, :, 4], u5[:, :, 0], u5[:, :, 4], u5[:, 0], u5[:, 4]]

def onehot(axis, index):
    shape = [1, 1, 1, 1, 1]
    shape[axis] = 5
    return (jnp.arange(5) == index).astype(jnp.float32).reshape(shape)

def residual(u5, outer, scale, lam):
    table = derivative_matrix()
    high = lax.Precision.HIGHEST
    div = jnp.einsum('ai,vkjie->vkjae', table, euler_flux(u5, 0), precision=high)
    div = div + jnp.einsum('aj,vkjie->vkaie', table, euler_flux(u5, 1), precision=high)
    div = div + jnp.einsum('ak,vkjie->vajie', table, euler_flux(u5, 2), precision=high)
    faces = own_faces(u5)
    correct = jnp.zeros_like(u5)
    for d in range(3):
        axis = 3 - d
        inner_low = faces[2 * d]
        inner_high = faces[2 * d + 1]
        lift_low = (rusanov(outer[2 * d], inner_low, d, lam) - euler_flux(inner_low, d)) / END_WEIGHT
        lift_high = (rusanov(inner_high, outer[2 * d + 1], d, lam) - euler_flux(inner_high, d)) / END_WEIGHT
        correct = correct + jnp.expand_dims(lift_low, axis) * onehot(axis, 0)
        correct = correct - jnp.expand_dims(lift_high, axis) * onehot(axis, 4)
    return scale * (correct - div)

def reference(state, levels, neighbours, shifts):
    total = ROWS * ECURVE
    u5 = state.reshape(NV, ORDER, ORDER, ORDER, total)
    scale = jnp.exp2(levels.reshape(total).astype(jnp.float32))
    speed = wave_speed(u5)
    lam = jnp.max(speed)
    top = jnp.max(speed * scale)
    faces = own_faces(u5)
    outer = []
    for f in range(6):
        opposite = faces[f + 1 - 2 * (f % 2)]
        outer.append(jnp.take(opposite, neighbours[f].reshape(total), axis=-1))
    new = u5 + CFL / top * residual(u5, outer, scale, lam)
    rowwise = new.reshape(NV, ORDER, ORDER, ORDER, ROWS, ECURVE)
    upper = rowwise[:, 4]
    before = jnp.roll(upper, 1, axis=-1)
    mflux = rusanov(before, rowwise[:, 0], 2, lam)
    position = jnp.arange(ECURVE, dtype=jnp.int32)
    block = position // EL
    source = (position[None, :] + shifts[:, block]) % ECURVE
    flat = (jnp.arange(ROWS, dtype=jnp.int32)[:, None] * ECURVE + source).astype(jnp.int32).reshape(-1)
    moved = jnp.take(new.reshape(NV * NODES, total), flat, axis=1).reshape(NV, NODES, ROWS, ECURVE)
    mortar = jnp.take(mflux.reshape(NV * FACE, total), flat, axis=1).reshape(NV, FACE, ROWS, ECURVE)
    return (moved, mortar)
```

```python
import functools

import jax
import jax.numpy as jnp
import ml_dtypes
import numpy as np
from jax import lax
from jax.experimental import pallas as pl
from jax.experimental.pallas import tpu as pltpu
from jax.sharding import PartitionSpec as P

NV = 5
ORDER = 5
NODES = 125
FACE = 25
NPAD = 128
FPAD = 32

GAMMA = 1.4
CFL = 0.05
END_WEIGHT = 0.1
BF16 = jnp.bfloat16
F32 = jnp.float32


def derivative_matrix():
    points = np.array([-1.0, -np.sqrt(3.0 / 7.0), 0.0, np.sqrt(3.0 / 7.0), 1.0])
    bary = np.array(
        [1.0 / np.prod([points[j] - points[k] for k in range(5) if k != j]) for j in range(5)]
    )
    table = np.zeros((5, 5))
    for i in range(5):
        for j in range(5):
            if i != j:
                table[i, j] = bary[j] / bary[i] / (points[i] - points[j])
        table[i, i] = -np.sum(table[i])
    return np.asarray(table, np.float32)


def face_nodes():
    n = np.arange(NODES).reshape(5, 5, 5)
    return [
        n[:, :, 0], n[:, :, 4], n[:, 0, :], n[:, 4, :], n[0], n[4],
    ]


def matrices():
    table = derivative_matrix()
    eye = np.eye(5, dtype=np.float32)
    per_dim = [
        np.kron(np.kron(eye, eye), table),
        np.kron(np.kron(eye, table), eye),
        np.kron(np.kron(table, eye), eye),
    ]
    wide = np.zeros((NPAD, 3 * NPAD), np.float32)
    for d in range(3):
        wide[:NODES, d * NPAD : d * NPAD + NODES] = -per_dim[d]
    high = wide.astype(ml_dtypes.bfloat16)
    low = (wide - high.astype(np.float32)).astype(ml_dtypes.bfloat16)
    signed = np.zeros((NPAD, 6 * FPAD), np.float32)
    plain = np.zeros((NPAD, 6 * FPAD), np.float32)
    half = 0.5 / END_WEIGHT
    for f, nodes in enumerate(face_nodes()):
        for r, n in enumerate(nodes.reshape(-1)):
            signed[n, f * FPAD + r] = half if f % 2 == 0 else -half
            plain[n, f * FPAD + r] = half
    div = np.concatenate([high, high, low], axis=1)
    signed = np.concatenate([signed, signed], axis=1).astype(ml_dtypes.bfloat16)
    plain = np.concatenate([plain, plain], axis=1).astype(ml_dtypes.bfloat16)
    return div, signed, plain


def primitive(u):
    inv = 1.0 / u[0]
    vel = [u[1] * inv, u[2] * inv, u[3] * inv]
    kinetic = u[1] * vel[0] + u[2] * vel[1] + u[3] * vel[2]
    press = (GAMMA - 1.0) * (u[4] - 0.5 * kinetic)
    return inv, vel, press


def flux(u, vel, press, d):
    along = vel[d]
    parts = [u[1 + d]]
    for a in range(3):
        term = u[1 + a] * along
        parts.append(term + press if a == d else term)
    parts.append((u[4] + press) * along)
    return parts


def flux_of(u, d):
    _, vel, press = primitive(u)
    return flux(u, vel, press, d)


def split(x, parts):
    out = []
    for p in range(parts):
        piece = x.astype(BF16)
        out.append(piece)
        if p < parts - 1:
            x = x - piece.astype(F32)
    return out


def mm(a, b):
    return jnp.dot(a, b, preferred_element_type=F32)


def pick(x, chosen):
    rows = x.shape[0]
    y = mm(jnp.concatenate(split(x, 3), axis=0), chosen)
    return y[:rows] + y[rows : 2 * rows] + y[2 * rows :]


def one_hot(rows, index):
    where = lax.broadcasted_iota(jnp.int32, (rows, index.shape[1]), 0)
    return jnp.where(where == index, 1.0, 0.0).astype(BF16)


def kernel(
    n_curve, n_slab,
    state_ref, ints_ref, div_ref, signed_ref, plain_ref,
    moved_ref, mortar_ref,
    faces, got, mine_s, mine_c, from_s, from_c, head, tail, got_head, got_tail, upper_ref,
    face_send, face_recv, s_send, s_recv, c_send, c_recv, halo_send, halo_recv,
):
    count = state_ref.shape[2]
    width = count // 4
    curve = lax.axis_index("curve")
    slab = lax.axis_index("slab")

    def on_curve(t):
        return {"curve": lax.rem(curve + t + n_curve, n_curve)}

    def on_slab(t):
        return {"slab": lax.rem(slab + t + n_slab, n_slab)}

    def remote(src, dst, send, recv, to):
        return pltpu.make_async_remote_copy(
            src_ref=src, dst_ref=dst, send_sem=send, recv_sem=recv,
            device_id=to, device_id_type=pl.DeviceIdType.MESH,
        )

    barrier = pltpu.get_barrier_semaphore()
    for t in range(1, n_slab):
        pl.semaphore_signal(barrier, inc=1, device_id=on_slab(t), device_id_type=pl.DeviceIdType.MESH)
    for t in range(1, n_curve):
        pl.semaphore_signal(barrier, inc=1, device_id=on_curve(t), device_id_type=pl.DeviceIdType.MESH)

    ones = jnp.ones((8, count), F32)
    for f in range(6):
        for v in range(NV):
            r = v * FPAD
            faces[f, r + 24 : r + 32, :] = ones
            if f < 2:
                faces[f, r : r + FACE, :] = state_ref[v, pl.ds(4 * f, FACE, stride=5), :]
            elif f < 4:
                for k in range(5):
                    n = 25 * k + 20 * (f - 2)
                    faces[f, r + 5 * k : r + 5 * k + 5, :] = state_ref[v, n : n + 5, :]
            else:
                n = 100 * (f - 4)
                faces[f, r : r + FACE, :] = state_ref[v, n : n + FACE, :]

    ints = ints_ref[...]
    scale = jnp.exp2(ints[6:7].astype(F32))
    u = [state_ref[v] for v in range(NV)]
    inv, vel, press = primitive(u)
    speed = jnp.sqrt(vel[0] * vel[0] + vel[1] * vel[1] + vel[2] * vel[2]) + jnp.sqrt(GAMMA * press * inv)
    node = lax.broadcasted_iota(jnp.int32, speed.shape, 0)
    fastest = jnp.max(jnp.where(node < NODES, speed, 0.0), axis=0, keepdims=True)
    row8 = lax.broadcasted_iota(jnp.int32, (8, count), 0)
    mine_s[...] = jnp.where(row8 == 0, fastest, fastest * scale)

    pl.semaphore_wait(barrier, n_slab + n_curve - 2)
    copies_s = []
    for t in range(1, n_slab):
        c = remote(mine_s, from_s.at[t - 1], s_send.at[t - 1], s_recv.at[t - 1], on_slab(t))
        c.start()
        copies_s.append(c)
    copies_f = [
        remote(faces.at[5], got.at[2], face_send.at[2], face_recv.at[2], on_curve(1)),
        remote(faces.at[4], got.at[3], face_send.at[3], face_recv.at[3], on_curve(-1)),
        remote(faces.at[1], got.at[0], face_send.at[0], face_recv.at[0], on_slab(1)),
        remote(faces.at[0], got.at[1], face_send.at[1], face_recv.at[1], on_slab(-1)),
    ]
    for c in copies_f:
        c.start()

    blocks = []
    for d in range(3):
        blocks.append(jnp.concatenate(flux(u, vel, press, d), axis=1))
    whole = jnp.concatenate(blocks, axis=0)
    whole_high, whole_low = split(whole, 2)

    for c in copies_s:
        c.wait()
    best = mine_s[...]
    for t in range(n_slab - 1):
        best = jnp.maximum(best, from_s[t])
    mine_c[...] = best
    copies_c = []
    for t in range(1, n_curve):
        c = remote(mine_c, from_c.at[t - 1], c_send.at[t - 1], c_recv.at[t - 1], on_curve(t))
        c.start()
        copies_c.append(c)

    total = mm(div_ref[...], jnp.concatenate([whole_high, whole_low, whole_high], axis=0))

    jumps, diffs = [None] * 6, [None] * 6

    def lift(f, outer):
        d = f // 2
        a = [faces[f, v * FPAD : (v + 1) * FPAD, :] for v in range(NV)]
        b = [outer[v * FPAD : (v + 1) * FPAD] for v in range(NV)]
        fa, fb = flux_of(a, d), flux_of(b, d)
        diffs[f] = jnp.concatenate([y - x for x, y in zip(fa, fb)], axis=1)
        jumps[f] = jnp.concatenate([y - x for x, y in zip(a, b)], axis=1)

    lift(2, pick(faces[3], one_hot(count, ints[2:3])))
    lift(3, pick(faces[2], one_hot(count, ints[3:4])))
    for g, f in ((0, 0), (1, 1)):
        copies_f[2 + g].wait()
        lift(f, pick(got[g], one_hot(count, ints[f : f + 1])))
    for g, f in ((2, 4), (3, 5)):
        copies_f[g - 2].wait()
        pair = jnp.concatenate([faces[9 - f], got[g]], axis=1)
        lift(f, pick(pair, one_hot(2 * count, ints[f : f + 1])))

    diff_all = jnp.concatenate(diffs, axis=0)
    jump_all = jnp.concatenate(jumps, axis=0)
    total = total + mm(signed_ref[...], jnp.concatenate(split(diff_all, 2), axis=0))
    spread = mm(plain_ref[...], jnp.concatenate(split(jump_all, 2), axis=0))

    for c in copies_c:
        c.wait()
    for t in range(n_curve - 1):
        best = jnp.maximum(best, from_c[t])
    peak = jnp.max(best, axis=1, keepdims=True)
    lam = peak[0:1]
    step = scale * (CFL / peak[1:2])

    lane = lax.broadcasted_iota(jnp.int32, (1, count), 1)
    part = lane // width
    new = []
    extra = jnp.zeros((FPAD, count), F32)
    for v in range(NV):
        cols = slice(v * count, (v + 1) * count)
        x = u[v] + step * (total[:, cols] + lam * spread[:, cols])
        new.append(x)
        packed_head, packed_tail = x[:FPAD], x[:FPAD]
        for g in range(1, 4):
            turned = pltpu.roll(x[g * FPAD : (g + 1) * FPAD], g * width, 1)
            packed_head = jnp.where(part == g, turned, packed_head)
            packed_tail = jnp.where(part == (3 + g) % 4, turned, packed_tail)
        head[v * FPAD : (v + 1) * FPAD, :] = packed_head
        tail[v * FPAD : (v + 1) * FPAD, :] = packed_tail
        last = pltpu.roll(x[3 * FPAD :], (v - (count - width - 1)) % count, 1)
        extra = jnp.where(lane == v, last, extra)
    tail[NV * FPAD :, :] = extra
    halo = [
        remote(tail, got_tail, halo_send.at[0], halo_recv.at[0], on_curve(1)),
        remote(head, got_head, halo_send.at[1], halo_recv.at[1], on_curve(-1)),
    ]
    for c in halo:
        c.start()

    shift = ints[7:8]

    def chosen(start):
        q = start + lane
        q = jnp.where(q < 0, q + count, jnp.where(q >= count, q - count, q))
        return one_hot(count, q), (lane < start) | (lane >= count + start)

    hot, foreign = chosen(shift)
    hot_before, foreign_before = chosen(shift - 1)
    for c in halo:
        c.wait()

    rows, rows_before = [], []
    extra = got_tail[NV * FPAD :, :]
    for v in range(NV):
        below = got_tail[v * FPAD : (v + 1) * FPAD, :]
        above = got_head[v * FPAD : (v + 1) * FPAD, :]
        for g in range(4):
            ends = jnp.where(part == g, above, below)
            if g:
                ends = pltpu.roll(ends, count - g * width, 1)
            own = new[v][g * FPAD : (g + 1) * FPAD]
            rows.append(jnp.where(foreign, ends, own))
        last = pltpu.roll(extra, count - width - 1 - v, 1)
        ends = jnp.where(lane == count - width - 1, last, ends)
        rows_before.append(jnp.where(foreign_before, ends, own))
    out = pick(jnp.concatenate(rows, axis=0), hot)
    for v in range(NV):
        moved_ref[v] = out[v * NPAD : v * NPAD + NODES]
    upper_ref[...] = pick(jnp.concatenate(rows_before, axis=0), hot_before)

    skip = NODES - FACE - 3 * FPAD
    lower = [upper_ref[v * FPAD + skip : v * FPAD + skip + FACE, :] for v in range(NV)]
    upper = [moved_ref[v, 0:FACE, :] for v in range(NV)]
    fl, fu = flux_of(lower, 2), flux_of(upper, 2)
    for v in range(NV):
        mortar_ref[v] = 0.5 * (fl[v] + fu[v]) - 0.5 * lam * (upper[v] - lower[v])


def on_device(n_curve, n_slab, state, levels, neighbours, shifts):
    count = state.shape[-1]
    padded = jnp.pad(
        state.reshape(NV, NODES, count), ((0, 0), (0, NPAD - NODES), (0, 0)), constant_values=1.0
    )
    local = neighbours.reshape(6, count)
    elsewhere = (local // count % n_curve != lax.axis_index("curve")).astype(jnp.int32) * count
    face = jnp.arange(6, dtype=jnp.int32)[:, None]
    slot = local % count + jnp.where(face >= 4, elsewhere, 0)
    ints = jnp.concatenate(
        [slot, levels.reshape(1, count), jnp.broadcast_to(shifts.reshape(1, 1), (1, count))], axis=0
    )
    div, signed, plain = matrices()
    vmem = pl.BlockSpec(memory_space=pltpu.VMEM)
    moved, mortar = pl.pallas_call(
        functools.partial(kernel, n_curve, n_slab),
        out_shape=(
            jax.ShapeDtypeStruct((NV, NODES, count), F32),
            jax.ShapeDtypeStruct((NV, FACE, count), F32),
        ),
        in_specs=[vmem] * 5,
        out_specs=(vmem, vmem),
        scratch_shapes=[
            pltpu.VMEM((6, NV * FPAD, count), F32),
            pltpu.VMEM((4, NV * FPAD, count), F32),
            pltpu.VMEM((8, count), F32),
            pltpu.VMEM((8, count), F32),
            pltpu.VMEM((n_slab - 1, 8, count), F32),
            pltpu.VMEM((n_curve - 1, 8, count), F32),
            pltpu.VMEM((NV * FPAD, count), F32),
            pltpu.VMEM((NV * FPAD + FPAD, count), F32),
            pltpu.VMEM((NV * FPAD, count), F32),
            pltpu.VMEM((NV * FPAD + FPAD, count), F32),
            pltpu.VMEM((NV * FPAD, count), F32),
            pltpu.SemaphoreType.DMA((4,)),
            pltpu.SemaphoreType.DMA((4,)),
            pltpu.SemaphoreType.DMA((n_slab - 1,)),
            pltpu.SemaphoreType.DMA((n_slab - 1,)),
            pltpu.SemaphoreType.DMA((n_curve - 1,)),
            pltpu.SemaphoreType.DMA((n_curve - 1,)),
            pltpu.SemaphoreType.DMA((2,)),
            pltpu.SemaphoreType.DMA((2,)),
        ],
        compiler_params=pltpu.CompilerParams(
            collective_id=0, has_side_effects=True, vmem_limit_bytes=32 * 1024 * 1024
        ),
        name="substep",
    )(padded, ints, jnp.asarray(div), jnp.asarray(signed), jnp.asarray(plain))
    return moved.reshape(NV, NODES, 1, count), mortar.reshape(NV, FACE, 1, count)


def solution(mesh):
    placed = (
        P(None, None, "slab", "curve"),
        P("slab", "curve"),
        P(None, "slab", "curve"),
        P("slab", "curve"),
    )
    return jax.shard_map(
        functools.partial(on_device, mesh.shape["curve"], mesh.shape["slab"]),
        mesh=mesh,
        in_specs=placed,
        out_specs=(P(None, None, "slab", "curve"), P(None, None, "slab", "curve")),
        check_vma=False,
    )
```

```python
import functools

import jax
import jax.numpy as jnp
import ml_dtypes
import numpy as np
from jax import lax
from jax.experimental import pallas as pl
from jax.experimental.pallas import tpu as pltpu
from jax.sharding import PartitionSpec as P

NV = 5
ORDER = 5
NODES = 125
FACE = 25
NPAD = 128
FPAD = 32

GAMMA = 1.4
CFL = 0.05
END_WEIGHT = 0.1
BF16 = jnp.bfloat16
F32 = jnp.float32


def derivative_matrix():
    points = np.array([-1.0, -np.sqrt(3.0 / 7.0), 0.0, np.sqrt(3.0 / 7.0), 1.0])
    bary = np.array(
        [1.0 / np.prod([points[j] - points[k] for k in range(5) if k != j]) for j in range(5)]
    )
    table = np.zeros((5, 5))
    for i in range(5):
        for j in range(5):
            if i != j:
                table[i, j] = bary[j] / bary[i] / (points[i] - points[j])
        table[i, i] = -np.sum(table[i])
    return np.asarray(table, np.float32)


def face_nodes():
    n = np.arange(NODES).reshape(5, 5, 5)
    return [
        n[:, :, 0], n[:, :, 4], n[:, 0, :], n[:, 4, :], n[0], n[4],
    ]


def matrices():
    table = derivative_matrix()
    eye = np.eye(5, dtype=np.float32)
    per_dim = [
        np.kron(np.kron(eye, eye), table),
        np.kron(np.kron(eye, table), eye),
        np.kron(np.kron(table, eye), eye),
    ]
    wide = np.zeros((NPAD, 3 * NPAD), np.float32)
    for d in range(3):
        wide[:NODES, d * NPAD : d * NPAD + NODES] = -per_dim[d]
    high = wide.astype(ml_dtypes.bfloat16)
    low = (wide - high.astype(np.float32)).astype(ml_dtypes.bfloat16)
    signed = np.zeros((NPAD, 6 * FPAD), np.float32)
    half = 0.5 / END_WEIGHT
    for f, nodes in enumerate(face_nodes()):
        for r, n in enumerate(nodes.reshape(-1)):
            signed[n, f * FPAD + r] = half if f % 2 == 0 else -half
    return np.concatenate([high, low], axis=1), signed.astype(ml_dtypes.bfloat16)


def primitive(u):
    inv = 1.0 / u[0]
    vel = [u[1] * inv, u[2] * inv, u[3] * inv]
    kinetic = u[1] * vel[0] + u[2] * vel[1] + u[3] * vel[2]
    press = (GAMMA - 1.0) * (u[4] - 0.5 * kinetic)
    return inv, vel, press


def flux(u, vel, press, d):
    along = vel[d]
    parts = [u[1 + d]]
    for a in range(3):
        term = u[1 + a] * along
        parts.append(term + press if a == d else term)
    parts.append((u[4] + press) * along)
    return parts


def flux_of(u, d):
    _, vel, press = primitive(u)
    return flux(u, vel, press, d)


def split(x, parts):
    out = []
    for p in range(parts):
        piece = x.astype(BF16)
        out.append(piece)
        if p < parts - 1:
            x = x - piece.astype(F32)
    return out


def mm(a, b):
    return jnp.dot(a, b, preferred_element_type=F32)


def pick(x, chosen):
    rows = x.shape[0]
    y = mm(jnp.concatenate(split(x, 3), axis=0), chosen)
    return y[:rows] + y[rows : 2 * rows] + y[2 * rows :]


def one_hot(rows, index):
    where = lax.broadcasted_iota(jnp.int32, (rows, index.shape[1]), 0)
    return jnp.where(where == index, 1.0, 0.0).astype(BF16)


def kernel(
    n_curve, n_slab,
    state_ref, levels_ref, neighbours_ref, shifts_ref, div_ref, signed_ref,
    moved_ref, mortar_ref,
    faces, got, mine_s, mine_c, from_s, from_c, head, tail, got_head, got_tail, upper_ref,
    face_send, face_recv, s_send, s_recv, c_send, c_recv, halo_send, halo_recv,
):
    count = state_ref.shape[2]
    width = count // 4
    curve = lax.axis_index("curve")
    slab = lax.axis_index("slab")

    def on_curve(t):
        return {"curve": lax.rem(curve + t + n_curve, n_curve)}

    def on_slab(t):
        return {"slab": lax.rem(slab + t + n_slab, n_slab)}

    def remote(src, dst, send, recv, to):
        return pltpu.make_async_remote_copy(
            src_ref=src, dst_ref=dst, send_sem=send, recv_sem=recv,
            device_id=to, device_id_type=pl.DeviceIdType.MESH,
        )

    barrier = pltpu.get_barrier_semaphore()
    for t in range(1, n_slab):
        pl.semaphore_signal(barrier, inc=1, device_id=on_slab(t), device_id_type=pl.DeviceIdType.MESH)
    for t in range(1, n_curve):
        pl.semaphore_signal(barrier, inc=1, device_id=on_curve(t), device_id_type=pl.DeviceIdType.MESH)

    ones = jnp.ones((8, count), F32)
    for f in range(6):
        for v in range(NV):
            r = v * FPAD
            faces[f, r + 24 : r + 32, :] = ones
            if f < 2:
                faces[f, r : r + FACE, :] = state_ref[v, pl.ds(4 * f, FACE, stride=5), :]
            elif f < 4:
                for k in range(5):
                    n = 25 * k + 20 * (f - 2)
                    faces[f, r + 5 * k : r + 5 * k + 5, :] = state_ref[v, n : n + 5, :]
            else:
                n = 100 * (f - 4)
                faces[f, r : r + FACE, :] = state_ref[v, n : n + FACE, :]

    u = [state_ref[v] for v in range(NV)]
    inv, vel, press = primitive(u)
    speed = jnp.sqrt(vel[0] * vel[0] + vel[1] * vel[1] + vel[2] * vel[2]) + jnp.sqrt(GAMMA * press * inv)
    node = lax.broadcasted_iota(jnp.int32, speed.shape, 0)
    fastest = jnp.max(jnp.where(node < NODES, speed, 0.0), axis=0, keepdims=True)
    scale = jnp.exp2(levels_ref[...].astype(F32))
    row8 = lax.broadcasted_iota(jnp.int32, (8, count), 0)
    mine_s[...] = jnp.where(row8 == 0, fastest, fastest * scale)

    pl.semaphore_wait(barrier, n_slab + n_curve - 2)
    copies_s = []
    for t in range(1, n_slab):
        c = remote(mine_s, from_s.at[t - 1], s_send.at[t - 1], s_recv.at[t - 1], on_slab(t))
        c.start()
        copies_s.append(c)
    copies_f = [
        remote(faces.at[5], got.at[2], face_send.at[2], face_recv.at[2], on_curve(1)),
        remote(faces.at[4], got.at[3], face_send.at[3], face_recv.at[3], on_curve(-1)),
        remote(faces.at[1], got.at[0], face_send.at[0], face_recv.at[0], on_slab(1)),
        remote(faces.at[0], got.at[1], face_send.at[1], face_recv.at[1], on_slab(-1)),
    ]
    for c in copies_f:
        c.start()

    blocks = []
    for d in range(3):
        blocks.append(jnp.concatenate(flux(u, vel, press, d), axis=1))
    whole = jnp.concatenate(blocks, axis=0)
    whole_high, whole_low = split(whole, 2)

    for c in copies_s:
        c.wait()
    best = mine_s[...]
    for t in range(n_slab - 1):
        best = jnp.maximum(best, from_s[t])
    mine_c[...] = best
    copies_c = []
    for t in range(1, n_curve):
        c = remote(mine_c, from_c.at[t - 1], c_send.at[t - 1], c_recv.at[t - 1], on_curve(t))
        c.start()
        copies_c.append(c)

    total = mm(div_ref[...], jnp.concatenate([whole_high, whole_high], axis=0))
    total = total + mm(div_ref[:, : 3 * NPAD], whole_low)

    jumps, diffs = [None] * 6, [None] * 6

    def lift(f, outer):
        d = f // 2
        a = [faces[f, v * FPAD : (v + 1) * FPAD, :] for v in range(NV)]
        b = [outer[v * FPAD : (v + 1) * FPAD] for v in range(NV)]
        fa, fb = flux_of(a, d), flux_of(b, d)
        diffs[f] = jnp.concatenate([y - x for x, y in zip(fa, fb)], axis=1)
        jumps[f] = jnp.concatenate([y - x for x, y in zip(a, b)], axis=1)

    def first(t_slab, t_curve):
        row = lax.rem(slab + t_slab + n_slab, n_slab)
        return (row * n_curve + lax.rem(curve + t_curve + n_curve, n_curve)) * count

    lift(2, pick(faces[3], one_hot(count, neighbours_ref[2] - first(0, 0))))
    lift(3, pick(faces[2], one_hot(count, neighbours_ref[3] - first(0, 0))))
    for g, t in ((0, -1), (1, 1)):
        hot = one_hot(count, neighbours_ref[g] - first(t, 0))
        copies_f[2 + g].wait()
        lift(g, pick(got[g], hot))
    for g, f, t in ((2, 4, -1), (3, 5, 1)):
        near = one_hot(count, neighbours_ref[f] - first(0, 0))
        far = one_hot(count, neighbours_ref[f] - first(0, t))
        hot = jnp.concatenate([near, far], axis=0)
        copies_f[g - 2].wait()
        lift(f, pick(jnp.concatenate([faces[9 - f], got[g]], axis=1), hot))

    diff_all = jnp.concatenate(diffs, axis=0)
    jump_all = jnp.concatenate(jumps, axis=0)
    signed = signed_ref[...]
    plain = jnp.abs(signed)
    diff_high, diff_low = split(diff_all, 2)
    jump_high, jump_low = split(jump_all, 2)
    total = total + (mm(signed, diff_high) + mm(signed, diff_low))
    spread = mm(plain, jump_high) + mm(plain, jump_low)

    for c in copies_c:
        c.wait()
    for t in range(n_curve - 1):
        best = jnp.maximum(best, from_c[t])
    peak = jnp.max(best, axis=1, keepdims=True)
    lam = peak[0:1]
    step = scale * (CFL / peak[1:2])

    lane = lax.broadcasted_iota(jnp.int32, (1, count), 1)
    part = lane // width
    new, halo = [], []
    extra = jnp.zeros((FPAD, count), F32)
    for v in range(NV):
        cols = slice(v * count, (v + 1) * count)
        x = u[v] + step * (total[:, cols] + lam * spread[:, cols])
        new.append(x)
        packed_head, packed_tail = x[:FPAD], x[:FPAD]
        for g in range(1, 4):
            turned = pltpu.roll(x[g * FPAD : (g + 1) * FPAD], g * width, 1)
            packed_head = jnp.where(part == g, turned, packed_head)
            packed_tail = jnp.where(part == (3 + g) % 4, turned, packed_tail)
        head[v * FPAD : (v + 1) * FPAD, :] = packed_head
        tail[v * FPAD : (v + 1) * FPAD, :] = packed_tail
        at = pl.ds(v * FPAD, FPAD)
        for i, (src, dst, t) in enumerate(((tail, got_tail, 1), (head, got_head, -1))):
            k = 2 * v + i
            c = remote(src.at[at], dst.at[at], halo_send.at[k], halo_recv.at[k], on_curve(t))
            c.start()
            halo.append(c)
        last = pltpu.roll(x[3 * FPAD :], (v - (count - width - 1)) % count, 1)
        extra = jnp.where(lane == v, last, extra)
    tail[NV * FPAD :, :] = extra
    at = pl.ds(NV * FPAD, FPAD)
    c = remote(tail.at[at], got_tail.at[at], halo_send.at[2 * NV], halo_recv.at[2 * NV], on_curve(1))
    c.start()
    halo.append(c)

    shift = shifts_ref[0, 0]

    def chosen(start):
        q = start + lane
        q = jnp.where(q < 0, q + count, jnp.where(q >= count, q - count, q))
        return one_hot(count, q), (lane < start) | (lane >= count + start)

    hot, foreign = chosen(shift)
    hot_before, foreign_before = chosen(shift - 1)
    corners = []
    for v in range(NV):
        halo[2 * v].wait()
        halo[2 * v + 1].wait()
        rows = []
        below = got_tail[v * FPAD : (v + 1) * FPAD, :]
        above = got_head[v * FPAD : (v + 1) * FPAD, :]
        for g in range(4):
            ends = jnp.where(part == g, above, below)
            if g:
                ends = pltpu.roll(ends, count - g * width, 1)
            own = new[v][g * FPAD : (g + 1) * FPAD]
            rows.append(jnp.where(foreign, ends, own))
        corners.append((ends, own))
        moved_ref[v] = pick(jnp.concatenate(rows, axis=0), hot)[:NODES]
    halo[2 * NV].wait()
    rows_before = []
    extra = got_tail[NV * FPAD :, :]
    for v in range(NV):
        ends, own = corners[v]
        last = pltpu.roll(extra, count - width - 1 - v, 1)
        ends = jnp.where(lane == count - width - 1, last, ends)
        rows_before.append(jnp.where(foreign_before, ends, own))
    upper_ref[...] = pick(jnp.concatenate(rows_before, axis=0), hot_before)

    skip = NODES - FACE - 3 * FPAD
    lower = [upper_ref[v * FPAD + skip : v * FPAD + skip + FACE, :] for v in range(NV)]
    upper = [moved_ref[v, 0:FACE, :] for v in range(NV)]
    fl, fu = flux_of(lower, 2), flux_of(upper, 2)
    for v in range(NV):
        mortar_ref[v] = 0.5 * (fl[v] + fu[v]) - 0.5 * lam * (upper[v] - lower[v])


def on_device(n_curve, n_slab, state, levels, neighbours, shifts):
    count = state.shape[-1]
    padded = jnp.pad(
        state.reshape(NV, NODES, count), ((0, 0), (0, NPAD - NODES), (0, 0)), constant_values=1.0
    )
    div, signed = matrices()
    vmem = pl.BlockSpec(memory_space=pltpu.VMEM)
    moved, mortar = pl.pallas_call(
        functools.partial(kernel, n_curve, n_slab),
        out_shape=(
            jax.ShapeDtypeStruct((NV, NODES, count), F32),
            jax.ShapeDtypeStruct((NV, FACE, count), F32),
        ),
        in_specs=[vmem] * 3 + [pl.BlockSpec(memory_space=pltpu.SMEM)] + [vmem] * 2,
        out_specs=(vmem, vmem),
        scratch_shapes=[
            pltpu.VMEM((6, NV * FPAD, count), F32),
            pltpu.VMEM((4, NV * FPAD, count), F32),
            pltpu.VMEM((8, count), F32),
            pltpu.VMEM((8, count), F32),
            pltpu.VMEM((n_slab - 1, 8, count), F32),
            pltpu.VMEM((n_curve - 1, 8, count), F32),
            pltpu.VMEM((NV * FPAD, count), F32),
            pltpu.VMEM((NV * FPAD + FPAD, count), F32),
            pltpu.VMEM((NV * FPAD, count), F32),
            pltpu.VMEM((NV * FPAD + FPAD, count), F32),
            pltpu.VMEM((NV * FPAD, count), F32),
            pltpu.SemaphoreType.DMA((4,)),
            pltpu.SemaphoreType.DMA((4,)),
            pltpu.SemaphoreType.DMA((n_slab - 1,)),
            pltpu.SemaphoreType.DMA((n_slab - 1,)),
            pltpu.SemaphoreType.DMA((n_curve - 1,)),
            pltpu.SemaphoreType.DMA((n_curve - 1,)),
            pltpu.SemaphoreType.DMA((2 * NV + 1,)),
            pltpu.SemaphoreType.DMA((2 * NV + 1,)),
        ],
        compiler_params=pltpu.CompilerParams(
            collective_id=0, has_side_effects=True, vmem_limit_bytes=32 * 1024 * 1024
        ),
        name="substep",
    )(padded, levels, neighbours, shifts, jnp.asarray(div), jnp.asarray(signed))
    return moved.reshape(NV, NODES, 1, count), mortar.reshape(NV, FACE, 1, count)


def solution(mesh):
    placed = (
        P(None, None, "slab", "curve"),
        P("slab", "curve"),
        P(None, "slab", "curve"),
        P("slab", "curve"),
    )
    return jax.shard_map(
        functools.partial(on_device, mesh.shape["curve"], mesh.shape["slab"]),
        mesh=mesh,
        in_specs=placed,
        out_specs=(P(None, None, "slab", "curve"), P(None, None, "slab", "curve")),
        check_vma=False,
    )
```

```python
import functools

import jax
import jax.numpy as jnp
import ml_dtypes
import numpy as np
from jax import lax
from jax.experimental import pallas as pl
from jax.experimental.pallas import tpu as pltpu
from jax.sharding import PartitionSpec as P

NV = 5
ORDER = 5
NODES = 125
FACE = 25
NPAD = 128
FPAD = 32

GAMMA = 1.4
CFL = 0.05
END_WEIGHT = 0.1
BF16 = jnp.bfloat16
F32 = jnp.float32


def derivative_matrix():
    points = np.array([-1.0, -np.sqrt(3.0 / 7.0), 0.0, np.sqrt(3.0 / 7.0), 1.0])
    bary = np.array(
        [1.0 / np.prod([points[j] - points[k] for k in range(5) if k != j]) for j in range(5)]
    )
    table = np.zeros((5, 5))
    for i in range(5):
        for j in range(5):
            if i != j:
                table[i, j] = bary[j] / bary[i] / (points[i] - points[j])
        table[i, i] = -np.sum(table[i])
    return np.asarray(table, np.float32)


def face_nodes():
    n = np.arange(NODES).reshape(5, 5, 5)
    return [
        n[:, :, 0], n[:, :, 4], n[:, 0, :], n[:, 4, :], n[0], n[4],
    ]


def matrices():
    table = derivative_matrix()
    eye = np.eye(5, dtype=np.float32)
    per_dim = [
        np.kron(np.kron(eye, eye), table),
        np.kron(np.kron(eye, table), eye),
        np.kron(np.kron(table, eye), eye),
    ]
    wide = np.zeros((NPAD, 3 * NPAD), np.float32)
    for d in range(3):
        wide[:NODES, d * NPAD : d * NPAD + NODES] = -per_dim[d]
    high = wide.astype(ml_dtypes.bfloat16)
    low = (wide - high.astype(np.float32)).astype(ml_dtypes.bfloat16)
    signed = np.zeros((NPAD, 6 * FPAD), np.float32)
    half = 0.5 / END_WEIGHT
    for f, nodes in enumerate(face_nodes()):
        for r, n in enumerate(nodes.reshape(-1)):
            signed[n, f * FPAD + r] = half if f % 2 == 0 else -half
    return np.concatenate([high, low], axis=1), signed.astype(ml_dtypes.bfloat16)


def primitive(u):
    inv = 1.0 / u[0]
    vel = [u[1] * inv, u[2] * inv, u[3] * inv]
    kinetic = u[1] * vel[0] + u[2] * vel[1] + u[3] * vel[2]
    press = (GAMMA - 1.0) * (u[4] - 0.5 * kinetic)
    return inv, vel, press


def flux(u, vel, press, d):
    along = vel[d]
    parts = [u[1 + d]]
    for a in range(3):
        term = u[1 + a] * along
        parts.append(term + press if a == d else term)
    parts.append((u[4] + press) * along)
    return parts


def flux_of(u, d):
    _, vel, press = primitive(u)
    return flux(u, vel, press, d)


def split(x, parts):
    out = []
    for p in range(parts):
        piece = x.astype(BF16)
        out.append(piece)
        if p < parts - 1:
            x = x - piece.astype(F32)
    return out


def mm(a, b):
    return jnp.dot(a, b, preferred_element_type=F32)


def pick(x, chosen):
    rows = x.shape[0]
    y = mm(jnp.concatenate(split(x, 2), axis=0), chosen)
    return y[:rows] + y[rows:]


def one_hot(rows, index):
    where = lax.broadcasted_iota(jnp.int32, (rows, index.shape[1]), 0)
    return jnp.where(where == index, 1.0, 0.0).astype(BF16)


def kernel(
    n_curve, n_slab,
    state_ref, levels_ref, neighbours_ref, shifts_ref, div_ref, signed_ref,
    moved_ref, mortar_ref,
    faces, got, mine_s, mine_c, from_s, from_c, head, tail, got_head, got_tail, upper_ref,
    face_send, face_recv, s_send, s_recv, c_send, c_recv, halo_send, halo_recv,
):
    count = state_ref.shape[2]
    width = count // 4
    curve = lax.axis_index("curve")
    slab = lax.axis_index("slab")

    def on_curve(t):
        return {"curve": lax.rem(curve + t + n_curve, n_curve)}

    def on_slab(t):
        return {"slab": lax.rem(slab + t + n_slab, n_slab)}

    def remote(src, dst, send, recv, to):
        return pltpu.make_async_remote_copy(
            src_ref=src, dst_ref=dst, send_sem=send, recv_sem=recv,
            device_id=to, device_id_type=pl.DeviceIdType.MESH,
        )

    barrier = pltpu.get_barrier_semaphore()
    for t in range(1, n_slab):
        pl.semaphore_signal(barrier, inc=1, device_id=on_slab(t), device_id_type=pl.DeviceIdType.MESH)
    for t in range(1, n_curve):
        pl.semaphore_signal(barrier, inc=1, device_id=on_curve(t), device_id_type=pl.DeviceIdType.MESH)

    ones = jnp.ones((8, count), F32)
    for f in range(6):
        for v in range(NV):
            r = v * FPAD
            faces[f, r + 24 : r + 32, :] = ones
            if f < 2:
                faces[f, r : r + FACE, :] = state_ref[v, pl.ds(4 * f, FACE, stride=5), :]
            elif f < 4:
                for k in range(5):
                    n = 25 * k + 20 * (f - 2)
                    faces[f, r + 5 * k : r + 5 * k + 5, :] = state_ref[v, n : n + 5, :]
            else:
                n = 100 * (f - 4)
                faces[f, r : r + FACE, :] = state_ref[v, n : n + FACE, :]

    u = [state_ref[v] for v in range(NV)]
    inv, vel, press = primitive(u)
    speed = jnp.sqrt(vel[0] * vel[0] + vel[1] * vel[1] + vel[2] * vel[2]) + jnp.sqrt(GAMMA * press * inv)
    node = lax.broadcasted_iota(jnp.int32, speed.shape, 0)
    fastest = jnp.max(jnp.where(node < NODES, speed, 0.0), axis=0, keepdims=True)
    scale = jnp.exp2(levels_ref[...].astype(F32))
    row8 = lax.broadcasted_iota(jnp.int32, (8, count), 0)
    mine_s[...] = jnp.where(row8 == 0, fastest, fastest * scale)

    pl.semaphore_wait(barrier, n_slab + n_curve - 2)
    copies_s = []
    for t in range(1, n_slab):
        c = remote(mine_s, from_s.at[t - 1], s_send.at[t - 1], s_recv.at[t - 1], on_slab(t))
        c.start()
        copies_s.append(c)
    copies_f = [
        remote(faces.at[5], got.at[2], face_send.at[2], face_recv.at[2], on_curve(1)),
        remote(faces.at[4], got.at[3], face_send.at[3], face_recv.at[3], on_curve(-1)),
        remote(faces.at[1], got.at[0], face_send.at[0], face_recv.at[0], on_slab(1)),
        remote(faces.at[0], got.at[1], face_send.at[1], face_recv.at[1], on_slab(-1)),
    ]
    for c in copies_f:
        c.start()

    blocks = []
    for d in range(3):
        blocks.append(jnp.concatenate(flux(u, vel, press, d), axis=1))
    whole = jnp.concatenate(blocks, axis=0)
    whole_high, whole_low = split(whole, 2)

    for c in copies_s:
        c.wait()
    best = mine_s[...]
    for t in range(n_slab - 1):
        best = jnp.maximum(best, from_s[t])
    mine_c[...] = best
    copies_c = []
    for t in range(1, n_curve):
        c = remote(mine_c, from_c.at[t - 1], c_send.at[t - 1], c_recv.at[t - 1], on_curve(t))
        c.start()
        copies_c.append(c)

    total = mm(div_ref[...], jnp.concatenate([whole_high, whole_high], axis=0))
    total = total + mm(div_ref[:, : 3 * NPAD], whole_low)

    jumps, diffs = [None] * 6, [None] * 6

    def lift(f, outer):
        d = f // 2
        a = [faces[f, v * FPAD : (v + 1) * FPAD, :] for v in range(NV)]
        b = [outer[v * FPAD : (v + 1) * FPAD] for v in range(NV)]
        fa, fb = flux_of(a, d), flux_of(b, d)
        diffs[f] = jnp.concatenate([y - x for x, y in zip(fa, fb)], axis=1)
        jumps[f] = jnp.concatenate([y - x for x, y in zip(a, b)], axis=1)

    def first(t_slab, t_curve):
        row = lax.rem(slab + t_slab + n_slab, n_slab)
        return (row * n_curve + lax.rem(curve + t_curve + n_curve, n_curve)) * count

    lift(2, pick(faces[3], one_hot(count, neighbours_ref[2] - first(0, 0))))
    lift(3, pick(faces[2], one_hot(count, neighbours_ref[3] - first(0, 0))))
    for g, t in ((0, -1), (1, 1)):
        hot = one_hot(count, neighbours_ref[g] - first(t, 0))
        copies_f[2 + g].wait()
        lift(g, pick(got[g], hot))
    for g, f, t in ((2, 4, -1), (3, 5, 1)):
        near = one_hot(count, neighbours_ref[f] - first(0, 0))
        far = one_hot(count, neighbours_ref[f] - first(0, t))
        hot = jnp.concatenate([near, far], axis=0)
        copies_f[g - 2].wait()
        lift(f, pick(jnp.concatenate([faces[9 - f], got[g]], axis=1), hot))

    diff_all = jnp.concatenate(diffs, axis=0)
    jump_all = jnp.concatenate(jumps, axis=0)
    signed = signed_ref[...]
    plain = jnp.abs(signed)
    diff_high, diff_low = split(diff_all, 2)
    jump_high, jump_low = split(jump_all, 2)
    total = total + (mm(signed, diff_high) + mm(signed, diff_low))
    spread = mm(plain, jump_high) + mm(plain, jump_low)

    for c in copies_c:
        c.wait()
    for t in range(n_curve - 1):
        best = jnp.maximum(best, from_c[t])
    peak = jnp.max(best, axis=1, keepdims=True)
    lam = peak[0:1]
    step = scale * (CFL / peak[1:2])

    lane = lax.broadcasted_iota(jnp.int32, (1, count), 1)
    part = lane // width
    new, halo = [], []
    extra = jnp.zeros((FPAD, count), F32)
    for v in range(NV):
        cols = slice(v * count, (v + 1) * count)
        x = u[v] + step * (total[:, cols] + lam * spread[:, cols])
        new.append(x)
        packed_head, packed_tail = x[:FPAD], x[:FPAD]
        for g in range(1, 4):
            turned = pltpu.roll(x[g * FPAD : (g + 1) * FPAD], g * width, 1)
            packed_head = jnp.where(part == g, turned, packed_head)
            packed_tail = jnp.where(part == (3 + g) % 4, turned, packed_tail)
        head[v * FPAD : (v + 1) * FPAD, :] = packed_head
        tail[v * FPAD : (v + 1) * FPAD, :] = packed_tail
        at = pl.ds(v * FPAD, FPAD)
        for i, (src, dst, t) in enumerate(((tail, got_tail, 1), (head, got_head, -1))):
            k = 2 * v + i
            c = remote(src.at[at], dst.at[at], halo_send.at[k], halo_recv.at[k], on_curve(t))
            c.start()
            halo.append(c)
        last = pltpu.roll(x[3 * FPAD :], (v - (count - width - 1)) % count, 1)
        extra = jnp.where(lane == v, last, extra)
    tail[NV * FPAD :, :] = extra
    at = pl.ds(NV * FPAD, FPAD)
    c = remote(tail.at[at], got_tail.at[at], halo_send.at[2 * NV], halo_recv.at[2 * NV], on_curve(1))
    c.start()
    halo.append(c)

    shift = shifts_ref[0, 0]

    def chosen(start):
        q = start + lane
        q = jnp.where(q < 0, q + count, jnp.where(q >= count, q - count, q))
        return one_hot(count, q), (lane < start) | (lane >= count + start)

    hot, foreign = chosen(shift)
    hot_before, foreign_before = chosen(shift - 1)
    corners = []
    for v in range(NV):
        halo[2 * v].wait()
        halo[2 * v + 1].wait()
        rows = []
        below = got_tail[v * FPAD : (v + 1) * FPAD, :]
        above = got_head[v * FPAD : (v + 1) * FPAD, :]
        for g in range(4):
            ends = jnp.where(part == g, above, below)
            if g:
                ends = pltpu.roll(ends, count - g * width, 1)
            own = new[v][g * FPAD : (g + 1) * FPAD]
            rows.append(jnp.where(foreign, ends, own))
        corners.append((ends, own))
        moved_ref[v] = pick(jnp.concatenate(rows, axis=0), hot)[:NODES]
    halo[2 * NV].wait()
    rows_before = []
    extra = got_tail[NV * FPAD :, :]
    for v in range(NV):
        ends, own = corners[v]
        last = pltpu.roll(extra, count - width - 1 - v, 1)
        ends = jnp.where(lane == count - width - 1, last, ends)
        rows_before.append(jnp.where(foreign_before, ends, own))
    upper_ref[...] = pick(jnp.concatenate(rows_before, axis=0), hot_before)

    skip = NODES - FACE - 3 * FPAD
    lower = [upper_ref[v * FPAD + skip : v * FPAD + skip + FACE, :] for v in range(NV)]
    upper = [moved_ref[v, 0:FACE, :] for v in range(NV)]
    fl, fu = flux_of(lower, 2), flux_of(upper, 2)
    for v in range(NV):
        mortar_ref[v] = 0.5 * (fl[v] + fu[v]) - 0.5 * lam * (upper[v] - lower[v])


def on_device(n_curve, n_slab, state, levels, neighbours, shifts):
    count = state.shape[-1]
    padded = jnp.pad(
        state.reshape(NV, NODES, count), ((0, 0), (0, NPAD - NODES), (0, 0)), constant_values=1.0
    )
    div, signed = matrices()
    vmem = pl.BlockSpec(memory_space=pltpu.VMEM)
    moved, mortar = pl.pallas_call(
        functools.partial(kernel, n_curve, n_slab),
        out_shape=(
            jax.ShapeDtypeStruct((NV, NODES, count), F32),
            jax.ShapeDtypeStruct((NV, FACE, count), F32),
        ),
        in_specs=[vmem] * 3 + [pl.BlockSpec(memory_space=pltpu.SMEM)] + [vmem] * 2,
        out_specs=(vmem, vmem),
        scratch_shapes=[
            pltpu.VMEM((6, NV * FPAD, count), F32),
            pltpu.VMEM((4, NV * FPAD, count), F32),
            pltpu.VMEM((8, count), F32),
            pltpu.VMEM((8, count), F32),
            pltpu.VMEM((n_slab - 1, 8, count), F32),
            pltpu.VMEM((n_curve - 1, 8, count), F32),
            pltpu.VMEM((NV * FPAD, count), F32),
            pltpu.VMEM((NV * FPAD + FPAD, count), F32),
            pltpu.VMEM((NV * FPAD, count), F32),
            pltpu.VMEM((NV * FPAD + FPAD, count), F32),
            pltpu.VMEM((NV * FPAD, count), F32),
            pltpu.SemaphoreType.DMA((4,)),
            pltpu.SemaphoreType.DMA((4,)),
            pltpu.SemaphoreType.DMA((n_slab - 1,)),
            pltpu.SemaphoreType.DMA((n_slab - 1,)),
            pltpu.SemaphoreType.DMA((n_curve - 1,)),
            pltpu.SemaphoreType.DMA((n_curve - 1,)),
            pltpu.SemaphoreType.DMA((2 * NV + 1,)),
            pltpu.SemaphoreType.DMA((2 * NV + 1,)),
        ],
        compiler_params=pltpu.CompilerParams(
            collective_id=0, has_side_effects=True, vmem_limit_bytes=32 * 1024 * 1024
        ),
        name="substep",
    )(padded, levels, neighbours, shifts, jnp.asarray(div), jnp.asarray(signed))
    return moved.reshape(NV, NODES, 1, count), mortar.reshape(NV, FACE, 1, count)


def solution(mesh):
    placed = (
        P(None, None, "slab", "curve"),
        P("slab", "curve"),
        P(None, "slab", "curve"),
        P("slab", "curve"),
    )
    return jax.shard_map(
        functools.partial(on_device, mesh.shape["curve"], mesh.shape["slab"]),
        mesh=mesh,
        in_specs=placed,
        out_specs=(P(None, None, "slab", "curve"), P(None, None, "slab", "curve")),
        check_vma=False,
    )
```

```python
import functools

import jax
import jax.numpy as jnp
import ml_dtypes
import numpy as np
from jax import lax
from jax.experimental import pallas as pl
from jax.experimental.pallas import tpu as pltpu
from jax.sharding import PartitionSpec as P

NV = 5
ORDER = 5
NODES = 125
FACE = 25
NPAD = 128
FPAD = 32

GAMMA = 1.4
CFL = 0.05
END_WEIGHT = 0.1
BF16 = jnp.bfloat16
F32 = jnp.float32


def derivative_matrix():
    points = np.array([-1.0, -np.sqrt(3.0 / 7.0), 0.0, np.sqrt(3.0 / 7.0), 1.0])
    bary = np.array(
        [1.0 / np.prod([points[j] - points[k] for k in range(5) if k != j]) for j in range(5)]
    )
    table = np.zeros((5, 5))
    for i in range(5):
        for j in range(5):
            if i != j:
                table[i, j] = bary[j] / bary[i] / (points[i] - points[j])
        table[i, i] = -np.sum(table[i])
    return np.asarray(table, np.float32)


def face_nodes():
    n = np.arange(NODES).reshape(5, 5, 5)
    return [
        n[:, :, 0], n[:, :, 4], n[:, 0, :], n[:, 4, :], n[0], n[4],
    ]


def matrices():
    table = derivative_matrix()
    eye = np.eye(5, dtype=np.float32)
    per_dim = [
        np.kron(np.kron(eye, eye), table),
        np.kron(np.kron(eye, table), eye),
        np.kron(np.kron(table, eye), eye),
    ]
    wide = np.zeros((NPAD, 3 * NPAD), np.float32)
    for d in range(3):
        wide[:NODES, d * NPAD : d * NPAD + NODES] = -per_dim[d]
    high = wide.astype(ml_dtypes.bfloat16)
    low = (wide - high.astype(np.float32)).astype(ml_dtypes.bfloat16)
    signed = np.zeros((NPAD, 6 * FPAD), np.float32)
    half = 0.5 / END_WEIGHT
    for f, nodes in enumerate(face_nodes()):
        for r, n in enumerate(nodes.reshape(-1)):
            signed[n, f * FPAD + r] = half if f % 2 == 0 else -half
    return np.concatenate([high, low], axis=1), signed.astype(ml_dtypes.bfloat16)


def primitive(u):
    inv = 1.0 / u[0]
    vel = [u[1] * inv, u[2] * inv, u[3] * inv]
    kinetic = u[1] * vel[0] + u[2] * vel[1] + u[3] * vel[2]
    press = (GAMMA - 1.0) * (u[4] - 0.5 * kinetic)
    return inv, vel, press


def flux(u, vel, press, d):
    along = vel[d]
    parts = [u[1 + d]]
    for a in range(3):
        term = u[1 + a] * along
        parts.append(term + press if a == d else term)
    parts.append((u[4] + press) * along)
    return parts


def flux_of(u, d):
    _, vel, press = primitive(u)
    return flux(u, vel, press, d)


def split(x, parts):
    out = []
    for p in range(parts):
        piece = x.astype(BF16)
        out.append(piece)
        if p < parts - 1:
            x = x - piece.astype(F32)
    return out


def mm(a, b):
    return jnp.dot(a, b, preferred_element_type=F32)


def pick(x, chosen):
    rows = x.shape[0]
    y = mm(jnp.concatenate(split(x, 3), axis=0), chosen)
    return y[:rows] + y[rows : 2 * rows] + y[2 * rows :]


def one_hot(rows, index):
    where = lax.broadcasted_iota(jnp.int32, (rows, index.shape[1]), 0)
    return jnp.where(where == index, 1.0, 0.0).astype(BF16)


def kernel(
    n_curve, n_slab,
    state_ref, levels_ref, neighbours_ref, shifts_ref, div_ref, signed_ref,
    moved_ref, mortar_ref,
    faces, got, mine_s, mine_c, from_s, from_c, head, tail, got_head, got_tail, upper_ref,
    face_send, face_recv, s_send, s_recv, c_send, c_recv, halo_send, halo_recv,
):
    count = state_ref.shape[2]
    width = count // 4
    curve = lax.axis_index("curve")
    slab = lax.axis_index("slab")

    def on_curve(t):
        return {"curve": lax.rem(curve + t + n_curve, n_curve)}

    def on_slab(t):
        return {"slab": lax.rem(slab + t + n_slab, n_slab)}

    def remote(src, dst, send, recv, to):
        return pltpu.make_async_remote_copy(
            src_ref=src, dst_ref=dst, send_sem=send, recv_sem=recv,
            device_id=to, device_id_type=pl.DeviceIdType.MESH,
        )

    barrier = pltpu.get_barrier_semaphore()
    for t in range(1, n_slab):
        pl.semaphore_signal(barrier, inc=1, device_id=on_slab(t), device_id_type=pl.DeviceIdType.MESH)
    for t in range(1, n_curve):
        pl.semaphore_signal(barrier, inc=1, device_id=on_curve(t), device_id_type=pl.DeviceIdType.MESH)

    ones = jnp.ones((8, count), F32)
    for f in range(6):
        for v in range(NV):
            r = v * FPAD
            faces[f, r + 24 : r + 32, :] = ones
            if f < 2:
                faces[f, r : r + FACE, :] = state_ref[v, pl.ds(4 * f, FACE, stride=5), :]
            elif f < 4:
                for k in range(5):
                    n = 25 * k + 20 * (f - 2)
                    faces[f, r + 5 * k : r + 5 * k + 5, :] = state_ref[v, n : n + 5, :]
            else:
                n = 100 * (f - 4)
                faces[f, r : r + FACE, :] = state_ref[v, n : n + FACE, :]

    u = [state_ref[v] for v in range(NV)]
    inv, vel, press = primitive(u)
    speed = jnp.sqrt(vel[0] * vel[0] + vel[1] * vel[1] + vel[2] * vel[2]) + jnp.sqrt(GAMMA * press * inv)
    node = lax.broadcasted_iota(jnp.int32, speed.shape, 0)
    fastest = jnp.max(jnp.where(node < NODES, speed, 0.0), axis=0, keepdims=True)
    scale = jnp.exp2(levels_ref[...].astype(F32))
    row8 = lax.broadcasted_iota(jnp.int32, (8, count), 0)
    mine_s[...] = jnp.where(row8 == 0, fastest, fastest * scale)

    pl.semaphore_wait(barrier, n_slab + n_curve - 2)
    copies_s = []
    for t in range(1, n_slab):
        c = remote(mine_s, from_s.at[t - 1], s_send.at[t - 1], s_recv.at[t - 1], on_slab(t))
        c.start()
        copies_s.append(c)
    copies_f = [
        remote(faces.at[5], got.at[2], face_send.at[2], face_recv.at[2], on_curve(1)),
        remote(faces.at[4], got.at[3], face_send.at[3], face_recv.at[3], on_curve(-1)),
        remote(faces.at[1], got.at[0], face_send.at[0], face_recv.at[0], on_slab(1)),
        remote(faces.at[0], got.at[1], face_send.at[1], face_recv.at[1], on_slab(-1)),
    ]
    for c in copies_f:
        c.start()

    blocks = []
    for d in range(3):
        blocks.append(jnp.concatenate(flux(u, vel, press, d), axis=1))
    whole = jnp.concatenate(blocks, axis=0)
    whole_high, whole_low = split(whole, 2)

    for c in copies_s:
        c.wait()
    best = mine_s[...]
    for t in range(n_slab - 1):
        best = jnp.maximum(best, from_s[t])
    mine_c[...] = best
    copies_c = []
    for t in range(1, n_curve):
        c = remote(mine_c, from_c.at[t - 1], c_send.at[t - 1], c_recv.at[t - 1], on_curve(t))
        c.start()
        copies_c.append(c)

    total = mm(div_ref[...], jnp.concatenate([whole_high, whole_high], axis=0))
    total = total + mm(div_ref[:, : 3 * NPAD], whole_low)

    jumps, diffs = [None] * 6, [None] * 6

    def lift(f, outer):
        d = f // 2
        a = [faces[f, v * FPAD : (v + 1) * FPAD, :] for v in range(NV)]
        b = [outer[v * FPAD : (v + 1) * FPAD] for v in range(NV)]
        fa, fb = flux_of(a, d), flux_of(b, d)
        diffs[f] = jnp.concatenate([y - x for x, y in zip(fa, fb)], axis=1)
        jumps[f] = jnp.concatenate([y - x for x, y in zip(a, b)], axis=1)

    def first(t_slab, t_curve):
        row = lax.rem(slab + t_slab + n_slab, n_slab)
        return (row * n_curve + lax.rem(curve + t_curve + n_curve, n_curve)) * count

    lift(2, pick(faces[3], one_hot(count, neighbours_ref[2] - first(0, 0))))
    lift(3, pick(faces[2], one_hot(count, neighbours_ref[3] - first(0, 0))))
    for g, t in ((0, -1), (1, 1)):
        hot = one_hot(count, neighbours_ref[g] - first(t, 0))
        copies_f[2 + g].wait()
        lift(g, pick(got[g], hot))
    for g, f, t in ((2, 4, -1), (3, 5, 1)):
        near = one_hot(count, neighbours_ref[f] - first(0, 0))
        far = one_hot(count, neighbours_ref[f] - first(0, t))
        hot = jnp.concatenate([near, far], axis=0)
        copies_f[g - 2].wait()
        lift(f, pick(jnp.concatenate([faces[9 - f], got[g]], axis=1), hot))

    diff_all = jnp.concatenate(diffs, axis=0)
    jump_all = jnp.concatenate(jumps, axis=0)
    signed = signed_ref[...]
    plain = jnp.abs(signed)
    diff_high, diff_low = split(diff_all, 2)
    jump_high, jump_low = split(jump_all, 2)
    total = total + (mm(signed, diff_high) + mm(signed, diff_low))
    spread = mm(plain, jump_high) + mm(plain, jump_low)

    for c in copies_c:
        c.wait()
    for t in range(n_curve - 1):
        best = jnp.maximum(best, from_c[t])
    peak = jnp.max(best, axis=1, keepdims=True)
    lam = peak[0:1]
    step = scale * (CFL / peak[1:2])

    lane = lax.broadcasted_iota(jnp.int32, (1, count), 1)
    part = lane // width
    new = []
    extra = jnp.zeros((FPAD, count), F32)
    for v in range(NV):
        cols = slice(v * count, (v + 1) * count)
        x = u[v] + step * (total[:, cols] + lam * spread[:, cols])
        new.append(x)
        packed_head, packed_tail = x[:FPAD], x[:FPAD]
        for g in range(1, 4):
            turned = pltpu.roll(x[g * FPAD : (g + 1) * FPAD], g * width, 1)
            packed_head = jnp.where(part == g, turned, packed_head)
            packed_tail = jnp.where(part == (3 + g) % 4, turned, packed_tail)
        head[v * FPAD : (v + 1) * FPAD, :] = packed_head
        tail[v * FPAD : (v + 1) * FPAD, :] = packed_tail
        last = pltpu.roll(x[3 * FPAD :], (v - (count - width - 1)) % count, 1)
        extra = jnp.where(lane == v, last, extra)
    tail[NV * FPAD :, :] = extra
    halo = [
        remote(tail, got_tail, halo_send.at[0], halo_recv.at[0], on_curve(1)),
        remote(head, got_head, halo_send.at[1], halo_recv.at[1], on_curve(-1)),
    ]
    for c in halo:
        c.start()

    shift = shifts_ref[0, 0]

    def chosen(start):
        q = start + lane
        q = jnp.where(q < 0, q + count, jnp.where(q >= count, q - count, q))
        return one_hot(count, q), (lane < start) | (lane >= count + start)

    hot, foreign = chosen(shift)
    hot_before, foreign_before = chosen(shift - 1)
    for c in halo:
        c.wait()

    rows, rows_before = [], []
    extra = got_tail[NV * FPAD :, :]
    for v in range(NV):
        below = got_tail[v * FPAD : (v + 1) * FPAD, :]
        above = got_head[v * FPAD : (v + 1) * FPAD, :]
        for g in range(4):
            ends = jnp.where(part == g, above, below)
            if g:
                ends = pltpu.roll(ends, count - g * width, 1)
            own = new[v][g * FPAD : (g + 1) * FPAD]
            rows.append(jnp.where(foreign, ends, own))
        last = pltpu.roll(extra, count - width - 1 - v, 1)
        ends = jnp.where(lane == count - width - 1, last, ends)
        rows_before.append(jnp.where(foreign_before, ends, own))
    out = pick(jnp.concatenate(rows, axis=0), hot)
    for v in range(NV):
        moved_ref[v] = out[v * NPAD : v * NPAD + NODES]
    upper_ref[...] = pick(jnp.concatenate(rows_before, axis=0), hot_before)

    skip = NODES - FACE - 3 * FPAD
    lower = [upper_ref[v * FPAD + skip : v * FPAD + skip + FACE, :] for v in range(NV)]
    upper = [moved_ref[v, 0:FACE, :] for v in range(NV)]
    fl, fu = flux_of(lower, 2), flux_of(upper, 2)
    for v in range(NV):
        mortar_ref[v] = 0.5 * (fl[v] + fu[v]) - 0.5 * lam * (upper[v] - lower[v])


def on_device(n_curve, n_slab, state, levels, neighbours, shifts):
    count = state.shape[-1]
    padded = jnp.pad(
        state.reshape(NV, NODES, count), ((0, 0), (0, NPAD - NODES), (0, 0)), constant_values=1.0
    )
    div, signed = matrices()
    vmem = pl.BlockSpec(memory_space=pltpu.VMEM)
    moved, mortar = pl.pallas_call(
        functools.partial(kernel, n_curve, n_slab),
        out_shape=(
            jax.ShapeDtypeStruct((NV, NODES, count), F32),
            jax.ShapeDtypeStruct((NV, FACE, count), F32),
        ),
        in_specs=[vmem] * 3 + [pl.BlockSpec(memory_space=pltpu.SMEM)] + [vmem] * 2,
        out_specs=(vmem, vmem),
        scratch_shapes=[
            pltpu.VMEM((6, NV * FPAD, count), F32),
            pltpu.VMEM((4, NV * FPAD, count), F32),
            pltpu.VMEM((8, count), F32),
            pltpu.VMEM((8, count), F32),
            pltpu.VMEM((n_slab - 1, 8, count), F32),
            pltpu.VMEM((n_curve - 1, 8, count), F32),
            pltpu.VMEM((NV * FPAD, count), F32),
            pltpu.VMEM((NV * FPAD + FPAD, count), F32),
            pltpu.VMEM((NV * FPAD, count), F32),
            pltpu.VMEM((NV * FPAD + FPAD, count), F32),
            pltpu.VMEM((NV * FPAD, count), F32),
            pltpu.SemaphoreType.DMA((4,)),
            pltpu.SemaphoreType.DMA((4,)),
            pltpu.SemaphoreType.DMA((n_slab - 1,)),
            pltpu.SemaphoreType.DMA((n_slab - 1,)),
            pltpu.SemaphoreType.DMA((n_curve - 1,)),
            pltpu.SemaphoreType.DMA((n_curve - 1,)),
            pltpu.SemaphoreType.DMA((2,)),
            pltpu.SemaphoreType.DMA((2,)),
        ],
        compiler_params=pltpu.CompilerParams(
            collective_id=0, has_side_effects=True, vmem_limit_bytes=32 * 1024 * 1024
        ),
        name="substep",
    )(padded, levels, neighbours, shifts, jnp.asarray(div), jnp.asarray(signed))
    return moved.reshape(NV, NODES, 1, count), mortar.reshape(NV, FACE, 1, count)


def solution(mesh):
    placed = (
        P(None, None, "slab", "curve"),
        P("slab", "curve"),
        P(None, "slab", "curve"),
        P("slab", "curve"),
    )
    return jax.shard_map(
        functools.partial(on_device, mesh.shape["curve"], mesh.shape["slab"]),
        mesh=mesh,
        in_specs=placed,
        out_specs=(P(None, None, "slab", "curve"), P(None, None, "slab", "curve")),
        check_vma=False,
    )
```

```python
import functools

import jax
import jax.numpy as jnp
import ml_dtypes
import numpy as np
from jax import lax
from jax.experimental import pallas as pl
from jax.experimental.pallas import tpu as pltpu
from jax.sharding import PartitionSpec as P

NV = 5
ORDER = 5
NODES = 125
FACE = 25
NPAD = 128
FPAD = 32

GAMMA = 1.4
CFL = 0.05
END_WEIGHT = 0.1
BF16 = jnp.bfloat16
F32 = jnp.float32


def derivative_matrix():
    points = np.array([-1.0, -np.sqrt(3.0 / 7.0), 0.0, np.sqrt(3.0 / 7.0), 1.0])
    bary = np.array(
        [1.0 / np.prod([points[j] - points[k] for k in range(5) if k != j]) for j in range(5)]
    )
    table = np.zeros((5, 5))
    for i in range(5):
        for j in range(5):
            if i != j:
                table[i, j] = bary[j] / bary[i] / (points[i] - points[j])
        table[i, i] = -np.sum(table[i])
    return np.asarray(table, np.float32)


def face_nodes():
    n = np.arange(NODES).reshape(5, 5, 5)
    return [
        n[:, :, 0], n[:, :, 4], n[:, 0, :], n[:, 4, :], n[0], n[4],
    ]


def matrices():
    table = derivative_matrix()
    eye = np.eye(5, dtype=np.float32)
    per_dim = [
        np.kron(np.kron(eye, eye), table),
        np.kron(np.kron(eye, table), eye),
        np.kron(np.kron(table, eye), eye),
    ]
    wide = np.zeros((NPAD, 3 * NPAD), np.float32)
    for d in range(3):
        wide[:NODES, d * NPAD : d * NPAD + NODES] = -per_dim[d]
    high = wide.astype(ml_dtypes.bfloat16)
    low = (wide - high.astype(np.float32)).astype(ml_dtypes.bfloat16)
    signed = np.zeros((NPAD, 6 * FPAD), np.float32)
    half = 0.5 / END_WEIGHT
    for f, nodes in enumerate(face_nodes()):
        for r, n in enumerate(nodes.reshape(-1)):
            signed[n, f * FPAD + r] = half if f % 2 == 0 else -half
    return np.concatenate([high, low], axis=1), signed.astype(ml_dtypes.bfloat16)


def primitive(u):
    inv = 1.0 / u[0]
    vel = [u[1] * inv, u[2] * inv, u[3] * inv]
    kinetic = u[1] * vel[0] + u[2] * vel[1] + u[3] * vel[2]
    press = (GAMMA - 1.0) * (u[4] - 0.5 * kinetic)
    return inv, vel, press


def flux(u, vel, press, d):
    along = vel[d]
    parts = [u[1 + d]]
    for a in range(3):
        term = u[1 + a] * along
        parts.append(term + press if a == d else term)
    parts.append((u[4] + press) * along)
    return parts


def flux_of(u, d):
    _, vel, press = primitive(u)
    return flux(u, vel, press, d)


def split(x, parts):
    out = []
    for p in range(parts):
        piece = x.astype(BF16)
        out.append(piece)
        if p < parts - 1:
            x = x - piece.astype(F32)
    return out


def mm(a, b):
    return jnp.dot(a, b, preferred_element_type=F32)


def pick(x, chosen):
    rows = x.shape[0]
    y = mm(jnp.concatenate(split(x, 3), axis=0), chosen)
    return y[:rows] + y[rows : 2 * rows] + y[2 * rows :]


def one_hot(rows, index):
    where = lax.broadcasted_iota(jnp.int32, (rows, index.shape[1]), 0)
    return jnp.where(where == index, 1.0, 0.0).astype(BF16)


def kernel(
    n_curve, n_slab,
    state_ref, levels_ref, neighbours_ref, shifts_ref, div_ref, signed_ref,
    moved_ref, mortar_ref,
    faces, got, mine_s, mine_c, from_s, from_c, head, tail, got_head, got_tail, upper_ref,
    face_send, face_recv, s_send, s_recv, c_send, c_recv, halo_send, halo_recv,
):
    count = state_ref.shape[2]
    width = count // 4
    curve = lax.axis_index("curve")
    slab = lax.axis_index("slab")

    def on_curve(t):
        return {"curve": lax.rem(curve + t + n_curve, n_curve)}

    def on_slab(t):
        return {"slab": lax.rem(slab + t + n_slab, n_slab)}

    def remote(src, dst, send, recv, to):
        return pltpu.make_async_remote_copy(
            src_ref=src, dst_ref=dst, send_sem=send, recv_sem=recv,
            device_id=to, device_id_type=pl.DeviceIdType.MESH,
        )

    barrier = pltpu.get_barrier_semaphore()
    for t in range(1, n_slab):
        pl.semaphore_signal(barrier, inc=1, device_id=on_slab(t), device_id_type=pl.DeviceIdType.MESH)
    for t in range(1, n_curve):
        pl.semaphore_signal(barrier, inc=1, device_id=on_curve(t), device_id_type=pl.DeviceIdType.MESH)

    ones = jnp.ones((8, count), F32)
    for f in range(6):
        for v in range(NV):
            r = v * FPAD
            faces[f, r + 24 : r + 32, :] = ones
            if f < 2:
                faces[f, r : r + FACE, :] = state_ref[v, pl.ds(4 * f, FACE, stride=5), :]
            elif f < 4:
                for k in range(5):
                    n = 25 * k + 20 * (f - 2)
                    faces[f, r + 5 * k : r + 5 * k + 5, :] = state_ref[v, n : n + 5, :]
            else:
                n = 100 * (f - 4)
                faces[f, r : r + FACE, :] = state_ref[v, n : n + FACE, :]

    pl.semaphore_wait(barrier, n_slab + n_curve - 2)
    copies_f = [
        remote(faces.at[5], got.at[2], face_send.at[2], face_recv.at[2], on_curve(1)),
        remote(faces.at[4], got.at[3], face_send.at[3], face_recv.at[3], on_curve(-1)),
        remote(faces.at[1], got.at[0], face_send.at[0], face_recv.at[0], on_slab(1)),
        remote(faces.at[0], got.at[1], face_send.at[1], face_recv.at[1], on_slab(-1)),
    ]
    for c in copies_f[:2]:
        c.start()

    u = [state_ref[v] for v in range(NV)]
    inv, vel, press = primitive(u)
    speed = jnp.sqrt(vel[0] * vel[0] + vel[1] * vel[1] + vel[2] * vel[2]) + jnp.sqrt(GAMMA * press * inv)
    node = lax.broadcasted_iota(jnp.int32, speed.shape, 0)
    fastest = jnp.max(jnp.where(node < NODES, speed, 0.0), axis=0, keepdims=True)
    scale = jnp.exp2(levels_ref[...].astype(F32))
    row8 = lax.broadcasted_iota(jnp.int32, (8, count), 0)
    mine_s[...] = jnp.where(row8 == 0, fastest, fastest * scale)

    copies_s = []
    for t in range(1, n_slab):
        c = remote(mine_s, from_s.at[t - 1], s_send.at[t - 1], s_recv.at[t - 1], on_slab(t))
        c.start()
        copies_s.append(c)
    for c in copies_f[2:]:
        c.start()

    blocks = []
    for d in range(3):
        blocks.append(jnp.concatenate(flux(u, vel, press, d), axis=1))
    whole = jnp.concatenate(blocks, axis=0)
    whole_high, whole_low = split(whole, 2)

    for c in copies_s:
        c.wait()
    best = mine_s[...]
    for t in range(n_slab - 1):
        best = jnp.maximum(best, from_s[t])
    mine_c[...] = best
    copies_c = []
    for t in range(1, n_curve):
        c = remote(mine_c, from_c.at[t - 1], c_send.at[t - 1], c_recv.at[t - 1], on_curve(t))
        c.start()
        copies_c.append(c)

    total = mm(div_ref[...], jnp.concatenate([whole_high, whole_high], axis=0))
    total = total + mm(div_ref[:, : 3 * NPAD], whole_low)

    jumps, diffs = [None] * 6, [None] * 6

    def lift(f, outer):
        d = f // 2
        a = [faces[f, v * FPAD : (v + 1) * FPAD, :] for v in range(NV)]
        b = [outer[v * FPAD : (v + 1) * FPAD] for v in range(NV)]
        fa, fb = flux_of(a, d), flux_of(b, d)
        diffs[f] = jnp.concatenate([y - x for x, y in zip(fa, fb)], axis=1)
        jumps[f] = jnp.concatenate([y - x for x, y in zip(a, b)], axis=1)

    def first(t_slab, t_curve):
        row = lax.rem(slab + t_slab + n_slab, n_slab)
        return (row * n_curve + lax.rem(curve + t_curve + n_curve, n_curve)) * count

    lift(2, pick(faces[3], one_hot(count, neighbours_ref[2] - first(0, 0))))
    lift(3, pick(faces[2], one_hot(count, neighbours_ref[3] - first(0, 0))))
    for g, t in ((0, -1), (1, 1)):
        hot = one_hot(count, neighbours_ref[g] - first(t, 0))
        copies_f[2 + g].wait()
        lift(g, pick(got[g], hot))
    for g, f, t in ((2, 4, -1), (3, 5, 1)):
        near = one_hot(count, neighbours_ref[f] - first(0, 0))
        far = one_hot(count, neighbours_ref[f] - first(0, t))
        hot = jnp.concatenate([near, far], axis=0)
        copies_f[g - 2].wait()
        lift(f, pick(jnp.concatenate([faces[9 - f], got[g]], axis=1), hot))

    diff_all = jnp.concatenate(diffs, axis=0)
    jump_all = jnp.concatenate(jumps, axis=0)
    signed = signed_ref[...]
    plain = jnp.abs(signed)
    diff_high, diff_low = split(diff_all, 2)
    jump_high, jump_low = split(jump_all, 2)
    total = total + (mm(signed, diff_high) + mm(signed, diff_low))
    spread = mm(plain, jump_high) + mm(plain, jump_low)

    for c in copies_c:
        c.wait()
    for t in range(n_curve - 1):
        best = jnp.maximum(best, from_c[t])
    peak = jnp.max(best, axis=1, keepdims=True)
    lam = peak[0:1]
    step = scale * (CFL / peak[1:2])

    lane = lax.broadcasted_iota(jnp.int32, (1, count), 1)
    part = lane // width
    new = []
    extra = jnp.zeros((FPAD, count), F32)
    for v in range(NV):
        cols = slice(v * count, (v + 1) * count)
        x = u[v] + step * (total[:, cols] + lam * spread[:, cols])
        new.append(x)
        packed_head, packed_tail = x[:FPAD], x[:FPAD]
        for g in range(1, 4):
            turned = pltpu.roll(x[g * FPAD : (g + 1) * FPAD], g * width, 1)
            packed_head = jnp.where(part == g, turned, packed_head)
            packed_tail = jnp.where(part == (3 + g) % 4, turned, packed_tail)
        head[v * FPAD : (v + 1) * FPAD, :] = packed_head
        tail[v * FPAD : (v + 1) * FPAD, :] = packed_tail
        last = pltpu.roll(x[3 * FPAD :], (v - (count - width - 1)) % count, 1)
        extra = jnp.where(lane == v, last, extra)
    tail[NV * FPAD :, :] = extra
    halo = [
        remote(tail, got_tail, halo_send.at[0], halo_recv.at[0], on_curve(1)),
        remote(head, got_head, halo_send.at[1], halo_recv.at[1], on_curve(-1)),
    ]
    for c in halo:
        c.start()

    shift = shifts_ref[0, 0]

    def chosen(start):
        q = start + lane
        q = jnp.where(q < 0, q + count, jnp.where(q >= count, q - count, q))
        return one_hot(count, q), (lane < start) | (lane >= count + start)

    hot, foreign = chosen(shift)
    hot_before, foreign_before = chosen(shift - 1)
    for c in halo:
        c.wait()

    rows, rows_before = [], []
    extra = got_tail[NV * FPAD :, :]
    for v in range(NV):
        below = got_tail[v * FPAD : (v + 1) * FPAD, :]
        above = got_head[v * FPAD : (v + 1) * FPAD, :]
        for g in range(4):
            ends = jnp.where(part == g, above, below)
            if g:
                ends = pltpu.roll(ends, count - g * width, 1)
            own = new[v][g * FPAD : (g + 1) * FPAD]
            rows.append(jnp.where(foreign, ends, own))
        last = pltpu.roll(extra, count - width - 1 - v, 1)
        ends = jnp.where(lane == count - width - 1, last, ends)
        rows_before.append(jnp.where(foreign_before, ends, own))
    out = pick(jnp.concatenate(rows, axis=0), hot)
    for v in range(NV):
        moved_ref[v] = out[v * NPAD : v * NPAD + NODES]
    upper_ref[...] = pick(jnp.concatenate(rows_before, axis=0), hot_before)

    skip = NODES - FACE - 3 * FPAD
    lower = [upper_ref[v * FPAD + skip : v * FPAD + skip + FACE, :] for v in range(NV)]
    upper = [moved_ref[v, 0:FACE, :] for v in range(NV)]
    fl, fu = flux_of(lower, 2), flux_of(upper, 2)
    for v in range(NV):
        mortar_ref[v] = 0.5 * (fl[v] + fu[v]) - 0.5 * lam * (upper[v] - lower[v])


def on_device(n_curve, n_slab, state, levels, neighbours, shifts):
    count = state.shape[-1]
    padded = jnp.pad(
        state.reshape(NV, NODES, count), ((0, 0), (0, NPAD - NODES), (0, 0)), constant_values=1.0
    )
    div, signed = matrices()
    vmem = pl.BlockSpec(memory_space=pltpu.VMEM)
    moved, mortar = pl.pallas_call(
        functools.partial(kernel, n_curve, n_slab),
        out_shape=(
            jax.ShapeDtypeStruct((NV, NODES, count), F32),
            jax.ShapeDtypeStruct((NV, FACE, count), F32),
        ),
        in_specs=[vmem] * 3 + [pl.BlockSpec(memory_space=pltpu.SMEM)] + [vmem] * 2,
        out_specs=(vmem, vmem),
        scratch_shapes=[
            pltpu.VMEM((6, NV * FPAD, count), F32),
            pltpu.VMEM((4, NV * FPAD, count), F32),
            pltpu.VMEM((8, count), F32),
            pltpu.VMEM((8, count), F32),
            pltpu.VMEM((n_slab - 1, 8, count), F32),
            pltpu.VMEM((n_curve - 1, 8, count), F32),
            pltpu.VMEM((NV * FPAD, count), F32),
            pltpu.VMEM((NV * FPAD + FPAD, count), F32),
            pltpu.VMEM((NV * FPAD, count), F32),
            pltpu.VMEM((NV * FPAD + FPAD, count), F32),
            pltpu.VMEM((NV * FPAD, count), F32),
            pltpu.SemaphoreType.DMA((4,)),
            pltpu.SemaphoreType.DMA((4,)),
            pltpu.SemaphoreType.DMA((n_slab - 1,)),
            pltpu.SemaphoreType.DMA((n_slab - 1,)),
            pltpu.SemaphoreType.DMA((n_curve - 1,)),
            pltpu.SemaphoreType.DMA((n_curve - 1,)),
            pltpu.SemaphoreType.DMA((2,)),
            pltpu.SemaphoreType.DMA((2,)),
        ],
        compiler_params=pltpu.CompilerParams(
            collective_id=0, has_side_effects=True, vmem_limit_bytes=32 * 1024 * 1024
        ),
        name="substep",
    )(padded, levels, neighbours, shifts, jnp.asarray(div), jnp.asarray(signed))
    return moved.reshape(NV, NODES, 1, count), mortar.reshape(NV, FACE, 1, count)


def solution(mesh):
    placed = (
        P(None, None, "slab", "curve"),
        P("slab", "curve"),
        P(None, "slab", "curve"),
        P("slab", "curve"),
    )
    return jax.shard_map(
        functools.partial(on_device, mesh.shape["curve"], mesh.shape["slab"]),
        mesh=mesh,
        in_specs=placed,
        out_specs=(P(None, None, "slab", "curve"), P(None, None, "slab", "curve")),
        check_vma=False,
    )
```
